512 devices in a mesh: expert: 128 (over y, z, core), dp: 4 (over x).
Axes of the slice: x: 4, y: 4, z: 16, core: 2. Of those that a mesh axis runs over, the one named last changes fastest.
Arguments:
- old_up: bfloat16 [128, 2048, 2, 512], P('expert', None, None, 'dp'), may hold values from -0.125 to 0.125
- old_down: bfloat16 [128, 2048, 2, 512], P('expert', None, None, 'dp'), may hold values from -0.1875 to 0.1875
- group_ids: int32 [128], replicated, may hold values from 0 to 63, as said below
- freq_counts: int32 [128], replicated, may hold values from 1 to 999
- tokens: bfloat16 [8192, 2048], P(('expert', 'dp')), may hold values from -6 to 6
- routing: int32 [8192, 8], P(('expert', 'dp')), may hold values from 0 to 63, all different within a row; in each aligned block of 16 rows (0 to 15, 16 to 31, ...) at most 4 rows name the same one
- probs: float32 [8192, 8], P(('expert', 'dp')), may hold values from 0.05 to 0.5
- cotangent: bfloat16 [8192, 2048], P(('expert', 'dp')), may hold values from -6 to 6
Outputs:
- layer_out: bfloat16 [8192, 2048], P(('expert', 'dp'))
- token_grad: bfloat16 [8192, 2048], P(('expert', 'dp'))
- gate_grad: float32 [8192, 8], P(('expert', 'dp'))
- up_grad: bfloat16 [128, 2048, 512], P('expert', None, 'dp')
- down_grad: bfloat16 [128, 2048, 512], P('expert', None, 'dp')
The draws below stay inside these ranges and needn't reach their ends.
Inputs may be any that keep to these rules, and one draw needn't show every extreme that they name: `group_ids`: each of the 64 merge groups holds 1 to 3 old experts, and some group holds exactly 3. `routing`: each token names 8 different merged experts; among the rows of one device no merged expert is named more than 4 times, and some device names one exactly 4 times.
All inputs are finite; a program needn't handle non-finite values.
Results may differ from the reference program's by a relative error of at most 0.022.
Values may be sent and summed in bfloat16 or wider, within the bound.
No kernel may reach another device: no remote copies, remote signals or barrier semaphores. Data moves between devices by JAX's collectives and lax.ppermute only.
A program may use at most 128 MiB of HBM per device.

```python
import math
import jax
import jax.numpy as jnp
import numpy as np
from jax import lax

D = 2048
F = 1024
TOK_DEV = 16
GMAX = 3
E_OLD = 128
E_NEW = 64
TOP = 8
MOST = 4
TOKENS = 8192
N_EXPERT = 128
N_DP = 4


def draw_group_ids(key, part):
    key = jax.random.fold_in(key, 11)
    key_first, key_heavy, key_label, key_spot = jax.random.split(key, 4)
    pair_count = E_NEW // 2
    first = jax.random.randint(key_first, (pair_count,), 1, 4).astype(jnp.int32)
    first = first.at[0].set(1 + 2 * jax.random.randint(key_heavy, (), 0, 2).astype(jnp.int32))
    sizes = jnp.stack([first, 4 - first], axis=1).reshape(-1)
    segment = jnp.repeat(jnp.arange(E_NEW, dtype=jnp.int32), sizes, total_repeat_length=E_OLD)
    relabel = jax.random.permutation(key_label, E_NEW).astype(jnp.int32)
    segment = relabel[segment]
    spots = jax.random.permutation(key_spot, E_OLD).astype(jnp.int32)
    return jnp.zeros((E_OLD,), jnp.int32).at[spots].set(segment)


def with_ends(values, rng, least, high):
    extent = values.shape
    index_at = [jax.random.randint(jax.random.fold_in(rng, axis), (), 0, extent[axis]) for axis in range(len(extent))]
    values = values.at[tuple(index_at)].set(least)
    longest = extent.index(max(extent))
    index_at[longest] = (index_at[longest] + 1) % extent[longest]
    return values.at[tuple(index_at)].set(high)


def shard_levels(own_key, dims, cuts, least, high):
    loudness = 1.0
    for axis_at, parts in cuts:
        heights = jax.random.uniform(jax.random.fold_in(jax.random.fold_in(own_key, 6), axis_at), (parts,), jnp.float32, least / len(cuts), high / len(cuts))
        loudness = loudness * jnp.repeat(jnp.exp(heights), dims[axis_at] // parts).reshape((-1,) + (1,) * (len(dims) - 1 - axis_at))
    return loudness


def shared_out(rng, own, number, rows, amount, top, reach, skew):
    ranking = jax.random.permutation(rng, amount)
    crowded, ordinary = load_shares(amount, rows * top, reach, skew, True), load_shares(amount, rows * top, reach, skew, False)
    places = jnp.arange(amount)

    def named(lengths, rotation):
        used = int((lengths > 0).sum())
        fixed = max(1, used // 4)
        shifted = fixed + (places - fixed + rotation * (used - fixed)) % max(1, amount - fixed)
        return jnp.zeros((amount,), jnp.int32).at[ranking[jnp.where(places < fixed, places, shifted)]].set(jnp.asarray(lengths, jnp.int32))

    lengths = jnp.where(number % 4 == 0, named(crowded, number // 4), named(ordinary, number - number // 4 - 1))
    mixed = jax.random.permutation(jax.random.fold_in(own, 3), amount)
    source_of, sink = mixed[0:amount // 2 * 2:2], mixed[1:amount // 2 * 2:2]
    margin = jnp.minimum(lengths[source_of] - 1, reach - lengths[sink]) // 2
    margin = jnp.where((source_of == ranking[0]) | (sink == ranking[0]) | (lengths[sink] == 0), 0, jnp.maximum(margin, 0))
    shifted = jax.random.randint(jax.random.fold_in(own, 4), (amount // 2,), 0, 1 << 20) % (margin + 1)
    lengths = lengths.at[source_of].add(-shifted).at[sink].add(shifted)
    items = jnp.searchsorted(jnp.cumsum(lengths), jnp.arange(rows * top), side="right").astype(jnp.int32)
    table = items.reshape(top, rows).T
    table = table[jax.random.permutation(jax.random.fold_in(own, 1), rows)]
    rotation = jax.random.randint(jax.random.fold_in(own, 2), (rows, 1), 0, top)
    return jnp.take_along_axis(table, (jnp.arange(top)[None, :] + rotation) % top, axis=1)


def load_shares(count, total, most, skew, full):
    loads = [(1 << 20) // math.isqrt(grade ** skew) + 1 for grade in range(1, count + 1)]
    largest = most if full else min(most, max(-(-total // count), total * loads[0] // sum(loads)))
    least = 1 if total - largest >= count - 1 else 0
    given, surplus = [largest] + [least] * (count - 1), total - largest - least * (count - 1)
    while surplus > 0:
        movable = [i for i in range(1, count) if given[i] < largest] or [i for i in range(1, count) if given[i] < most]
        whole, budget = sum([loads[i] for i in movable]), surplus
        for i in movable:
            extra = min(most - given[i], max(1, budget * loads[i] // whole), surplus)
            given[i] = given[i] + extra
            surplus = surplus - extra
    return np.array(given)


def gaussian(stream_key, dims, scale, limit, cuts=(), kind=jnp.bfloat16):
    entries = scale * jax.random.normal(stream_key, dims, jnp.float32)
    if cuts:
        entries = entries * shard_levels(stream_key, dims, cuts, -0.22, 0.18)
    return jnp.clip(entries, -limit, limit).astype(kind)


def setup_inputs(seed: int = 0) -> dict:
    seeds = jax.random.split(jax.random.key(seed), 9)
    old_up = gaussian(seeds[0], (E_OLD, D, 2, F // 2), D ** -0.5, 0.125, ((0, 128), (3, 4)))
    old_down = gaussian(seeds[1], (E_OLD, D, 2, F // 2), F ** -0.5, 0.1875, ((0, 128), (3, 4)))
    group_ids = draw_group_ids(jax.random.fold_in(seeds[8], 71), 0)
    freq_counts = with_ends(jax.random.randint(seeds[3], (E_OLD,), 1, 1000), jax.random.fold_in(seeds[3], 1), 1, 999).astype(jnp.int32)
    tokens = gaussian(seeds[4], (TOKENS, D), 1.0, 6.0, ((0, 512),))
    routing_keys = jax.random.split(jax.random.fold_in(seeds[5], 1), TOKENS // TOK_DEV)
    routing_turns = jax.random.permutation(jax.random.fold_in(seeds[5], 3), TOKENS // TOK_DEV)
    routing = jax.vmap(lambda own, number: shared_out(jax.random.fold_in(seeds[5], 2), own, number, TOK_DEV, E_NEW, TOP, MOST, 1))(routing_keys, routing_turns).reshape((TOKENS, TOP))
    probs = jnp.clip(0.05 + 0.45 * jax.random.uniform(seeds[6], (TOKENS, TOP), jnp.float32) ** shard_levels(seeds[6], (TOKENS, TOP), ((0, 512),), -0.2, 0.2), 0.05, 0.5)
    cotangent = gaussian(seeds[7], (TOKENS, D), 1.0, 6.0, ((0, 512),))
    return {"old_up": old_up, "old_down": old_down, "group_ids": group_ids, "freq_counts": freq_counts, "tokens": tokens, "routing": routing, "probs": probs, "cotangent": cotangent}


def silu_parts(preact):
    sigmoid_act = jax.nn.sigmoid(preact)
    return preact * sigmoid_act, sigmoid_act * (1.0 + preact * (1.0 - sigmoid_act))


def reference(old_up, old_down, group_ids, freq_counts, tokens, routing, probs, cotangent):
    member = (group_ids[None, :] == jnp.arange(E_NEW, dtype=jnp.int32)[:, None]).astype(jnp.int32)
    rank = jnp.sum((jnp.cumsum(member, axis=1) - member) * member, axis=0)
    weights = freq_counts.astype(jnp.float32)
    totals = jnp.sum(member.astype(jnp.float32) * weights[None, :], axis=1)
    merge_coef = member.astype(jnp.float32) * weights[None, :] / totals[:, None]
    select = member[:, None, :] * (rank[None, None, :] == jnp.arange(GMAX, dtype=jnp.int32)[None, :, None]).astype(jnp.int32)
    index_table = jnp.sum(select * jnp.arange(E_OLD, dtype=jnp.int32)[None, None, :], axis=2).astype(jnp.int32)
    coef_table = jnp.sum(select.astype(jnp.float32) * merge_coef[:, None, :], axis=2)

    def merge_one(entry):
        members, factors = entry
        total_up = jnp.zeros((D, 2, F // 2), jnp.float32)
        total_down = jnp.zeros((D, 2, F // 2), jnp.float32)
        for slot in range(GMAX):
            total_up = total_up + factors[slot] * old_up[members[slot]].astype(jnp.float32)
            total_down = total_down + factors[slot] * old_down[members[slot]].astype(jnp.float32)
        return total_up.astype(jnp.bfloat16).reshape(D, F), total_down.astype(jnp.bfloat16).reshape(D, F)

    merged_up, merged_down = lax.map(merge_one, (index_table, coef_table))

    total_pairs = TOKENS * TOP
    flat = routing.reshape(-1).astype(jnp.int32)
    row_dp = (jnp.arange(total_pairs, dtype=jnp.int32) // TOP // TOK_DEV) % N_DP
    sort_key = flat * N_DP + row_dp
    order = jnp.argsort(sort_key, stable=True).astype(jnp.int32)
    counts = jnp.zeros((E_NEW * N_DP,), jnp.int32).at[sort_key].add(1)
    starts = (jnp.cumsum(counts) - counts).astype(jnp.int32)
    capacity = N_EXPERT * MOST
    order_pad = jnp.concatenate([order, jnp.zeros((capacity,), jnp.int32)])
    prob_flat = probs.reshape(-1)
    half = F // 2

    def per_expert(carry, expert):
        out_acc, grad_acc, gate_acc = carry
        w_up = merged_up[expert]
        w_down = merged_down[expert]
        up_total = jnp.zeros((D, F), jnp.float32)
        down_total = jnp.zeros((D, F), jnp.float32)
        for shard in range(N_DP):
            block_key = expert * N_DP + shard
            picked = lax.dynamic_slice(order_pad, (starts[block_key].astype(jnp.int32),), (capacity,))
            valid = jnp.arange(capacity, dtype=jnp.int32) < counts[block_key]
            token_idx = picked // TOP
            rows_x = tokens[token_idx]
            grad_in = cotangent[token_idx].astype(jnp.float32)
            rows_p = jnp.where(valid, prob_flat[picked], 0.0).astype(jnp.float32)
            preact = jnp.dot(rows_x, w_up, preferred_element_type=jnp.float32)
            act_value, act_slope = silu_parts(preact)
            hidden = act_value.astype(jnp.bfloat16)
            out_grad = (rows_p[:, None] * grad_in).astype(jnp.bfloat16)
            hidden_grad = jnp.dot(out_grad, w_down, preferred_element_type=jnp.float32)
            act_grad = (hidden_grad * act_slope).astype(jnp.bfloat16)
            out_add = jnp.zeros((capacity, D), jnp.float32)
            grad_add = jnp.zeros((capacity, D), jnp.float32)
            gate_add = jnp.zeros((capacity,), jnp.float32)
            for part in range(2):
                cols = slice(part * half, (part + 1) * half)
                full_h = jnp.dot(hidden[:, cols], w_down[:, cols].T, preferred_element_type=jnp.float32)
                weighted_h = lax.optimization_barrier((rows_p[:, None] * full_h).astype(jnp.bfloat16))
                out_add = out_add + weighted_h.astype(jnp.float32)
                gate_add = gate_add + jnp.sum(full_h * grad_in, axis=1)
                input_h = jnp.dot(act_grad[:, cols], w_up[:, cols].T, preferred_element_type=jnp.float32)
                input_h = lax.optimization_barrier(input_h.astype(jnp.bfloat16))
                grad_add = grad_add + input_h.astype(jnp.float32)
            out_acc = out_acc.at[token_idx].add(out_add)
            grad_acc = grad_acc.at[token_idx].add(grad_add)
            gate_acc = gate_acc.at[picked].add(jnp.where(valid, gate_add, 0.0))
            up_part = lax.optimization_barrier(jnp.dot(rows_x.T, act_grad, preferred_element_type=jnp.float32).astype(jnp.bfloat16))
            down_part = lax.optimization_barrier(jnp.dot(out_grad.T, hidden, preferred_element_type=jnp.float32).astype(jnp.bfloat16))
            up_total = up_total + up_part.astype(jnp.float32)
            down_total = down_total + down_part.astype(jnp.float32)
        return (out_acc, grad_acc, gate_acc), (up_total.astype(jnp.bfloat16), down_total.astype(jnp.bfloat16))

    start_carry = (jnp.zeros((TOKENS, D), jnp.float32), jnp.zeros((TOKENS, D), jnp.float32), jnp.zeros((total_pairs,), jnp.float32))
    final, stacked = lax.scan(per_expert, start_carry, jnp.arange(E_NEW, dtype=jnp.int32))
    out_acc, grad_acc, gate_acc = final
    up_stack, down_stack = stacked

    def by_halves(grads):
        return grads.reshape(E_NEW, D, 2, half).transpose(0, 2, 1, 3).reshape(2 * E_NEW, D, half)

    return (out_acc.astype(jnp.bfloat16), grad_acc.astype(jnp.bfloat16), gate_acc.reshape(TOKENS, TOP), by_halves(up_stack), by_halves(down_stack))
```

```python
import jax
import jax.numpy as jnp
from jax import lax
from jax.experimental import pallas as pl
from jax.experimental.pallas import tpu as pltpu
from jax.sharding import Mesh
from jax.sharding import PartitionSpec as P

GMAX = 3
SLOTS = 4
BF = jnp.bfloat16
F32 = jnp.float32


def merge_kernel(index_ref, coef_ref, rows_ref, out_ref):
    groups = out_ref.shape[0]

    def one(g, carry):
        total = coef_ref[GMAX * g] * rows_ref[index_ref[GMAX * g]].astype(F32)
        for m in range(1, GMAX):
            total = total + coef_ref[GMAX * g + m] * rows_ref[index_ref[GMAX * g + m]].astype(F32)
        out_ref[g] = total.astype(BF)
        return carry

    lax.fori_loop(0, groups, one, 0, unroll=4)


def merge(index_table, coef_table, rows):
    groups = index_table.shape[0]
    shape = (groups,) + rows.shape[1:]
    return pl.pallas_call(
        merge_kernel,
        out_shape=jax.ShapeDtypeStruct(shape, BF),
        in_specs=[
            pl.BlockSpec(memory_space=pltpu.SMEM),
            pl.BlockSpec(memory_space=pltpu.SMEM),
            pl.BlockSpec(memory_space=pltpu.VMEM),
        ],
        out_specs=pl.BlockSpec(memory_space=pltpu.VMEM),
        compiler_params=pltpu.CompilerParams(vmem_limit_bytes=24 * 2**20),
        cost_estimate=pl.CostEstimate(
            flops=0, bytes_accessed=2 * rows.size + 2 * groups * rows[0].size, transcendentals=0
        ),
    )(index_table.reshape(-1), coef_table.reshape(-1), rows)


def shards(old_up, old_down, group_ids, freq_counts, tokens, routing, probs, cotangent):
    chips = lax.axis_size("chip")
    groups = chips
    width = tokens.shape[1]
    token_rows, chosen = routing.shape
    block = width // chips
    quarter = old_up.shape[3]
    both = ("chip", "core")

    member = (group_ids[None, :] == jnp.arange(groups, dtype=jnp.int32)[:, None]).astype(jnp.int32)
    rank = jnp.sum((jnp.cumsum(member, axis=1) - member) * member, axis=0)
    weights = freq_counts.astype(F32)
    totals = jnp.sum(member.astype(F32) * weights[None, :], axis=1)
    merge_coef = member.astype(F32) * weights[None, :] / totals[:, None]
    select = member[:, None, :] * (
        rank[None, None, :] == jnp.arange(GMAX, dtype=jnp.int32)[None, :, None]
    ).astype(jnp.int32)
    index_table = jnp.sum(
        select * jnp.arange(member.shape[1], dtype=jnp.int32)[None, None, :], axis=2
    ).astype(jnp.int32)
    coef_table = jnp.sum(select.astype(F32) * merge_coef[:, None, :], axis=2)

    def by_owner(w):
        return w.reshape(chips, block, 2, quarter).transpose(0, 2, 1, 3)

    spread = jnp.concatenate([by_owner(old_up), by_owner(old_down)], axis=2)
    spread = spread.reshape(2 * chips, 2 * block, quarter)
    spread = lax.all_to_all(spread, both, split_axis=0, concat_axis=0, tiled=True)
    merged = merge(index_table, coef_table, spread)
    merged = lax.all_to_all(merged, "chip", split_axis=0, concat_axis=0, tiled=True)
    up_half = merged[:, :block].reshape(width, quarter)
    down_half = merged[:, block:].reshape(width, quarter)
    w_up = lax.all_gather(up_half, "dp", axis=1, tiled=True)
    w_down = lax.all_gather(down_half, "dp", axis=1, tiled=True)

    flat = routing.reshape(-1)
    onehot = (flat[:, None] == jnp.arange(groups, dtype=jnp.int32)[None, :]).astype(jnp.int32)
    order_rank = jnp.sum((jnp.cumsum(onehot, axis=0) - onehot) * onehot, axis=1)
    slot_of = (flat * (2 * SLOTS) + order_rank).reshape(token_rows, chosen)
    places = groups * 2 * SLOTS
    place = jnp.arange(places, dtype=jnp.int32)
    hit_x = place[:, None, None] == slot_of[None]
    hit_g = place[:, None, None] == slot_of[None] + SLOTS
    map_x = jnp.any(hit_x, axis=2).astype(BF)
    map_g = jnp.any(hit_g, axis=2).astype(BF)
    row_p = jnp.sum(jnp.where(hit_g, probs[None], 0.0), axis=(1, 2))
    factor = jnp.where((place // SLOTS) % 2 == 0, 1.0, row_p)
    pick = jnp.concatenate([map_x, map_g], axis=1)
    both_rows = jnp.concatenate([tokens, cotangent], axis=0)
    send = (jnp.dot(pick, both_rows, preferred_element_type=F32) * factor[:, None]).astype(BF)
    send = send.reshape(groups, 2 * SLOTS, width)
    send, merged = lax.optimization_barrier((send, merged))
    recv = lax.all_to_all(send, "chip", split_axis=0, concat_axis=0, tiled=True)
    swap = [(0, 1), (1, 0)]
    other = lax.ppermute(recv, "core", swap)
    per = chips * 2 * SLOTS
    rows = jnp.concatenate([recv.reshape(per, width), other.reshape(per, width)], axis=0)

    is_x = ((jnp.arange(2 * per, dtype=jnp.int32) // SLOTS) % 2 == 0)[:, None]
    preact = jnp.dot(rows, w_up, preferred_element_type=F32)
    hidden_grad = jnp.dot(rows, w_down, preferred_element_type=F32)

    def to_other(v):
        return jnp.roll(v.reshape(-1, 2 * SLOTS, v.shape[1]), SLOTS, axis=1).reshape(v.shape)

    sig = jax.nn.sigmoid(preact)
    hidden = jnp.where(is_x, preact * sig, 0.0)
    slope = sig * (1.0 + preact * (1.0 - sig))
    act_grad = jnp.where(is_x, to_other(hidden_grad) * slope, 0.0)
    hidden_g = to_other(hidden).astype(BF)
    act_grad_g = to_other(act_grad).astype(BF)
    hidden = hidden.astype(BF)
    act_grad = act_grad.astype(BF)
    last = (((1,), (1,)), ((), ()))
    first = (((0,), (0,)), ((), ()))
    result = lax.dot_general(hidden, w_down, last, preferred_element_type=F32) + lax.dot_general(
        act_grad_g, w_up, last, preferred_element_type=F32
    )
    mine, theirs = result[:per], result[per:].astype(BF)
    back = mine + lax.ppermute(theirs, "core", swap).astype(F32)
    back = back.astype(BF).reshape(groups, 2 * SLOTS, width)
    back = lax.all_to_all(back, "chip", split_axis=0, concat_axis=0, tiled=True)
    back = back.reshape(places, width)

    up_part = lax.dot_general(rows, act_grad, first, preferred_element_type=F32).astype(BF)
    down_part = lax.dot_general(rows, hidden_g, first, preferred_element_type=F32).astype(BF)
    up_share = lax.psum_scatter(up_part, "dp", scatter_dimension=1, tiled=True)
    down_share = lax.psum_scatter(down_part, "dp", scatter_dimension=1, tiled=True)

    with_p = jnp.sum(jnp.where(hit_x, probs[None], 0.0), axis=2).T
    p_high = with_p.astype(BF)
    p_low = (with_p - p_high.astype(F32)).astype(BF)
    gather = jnp.concatenate([p_high, p_low, map_g.T], axis=0)
    sums = jnp.dot(gather, back, preferred_element_type=F32)
    layer_out = (sums[:token_rows] + sums[token_rows : 2 * token_rows]).astype(BF)
    token_grad = sums[2 * token_rows :].astype(BF)
    gates = lax.dot_general(cotangent, back, last, preferred_element_type=F32)
    gate_grad = jnp.sum(
        jnp.where(slot_of[:, :, None] == place[None, None, :], gates[:, None, :], 0.0), axis=2
    )
    return layer_out, token_grad, gate_grad, up_share[None], down_share[None]


def solution(mesh):
    experts, data = mesh.devices.shape
    fine = Mesh(mesh.devices.reshape(experts // 2, 2, data), ("chip", "core", "dp"))
    expert = ("chip", "core")
    rows = ("chip", "core", "dp")
    in_specs = (
        P(expert, None, None, "dp"),
        P(expert, None, None, "dp"),
        P(),
        P(),
        P(rows, None),
        P(rows, None),
        P(rows, None),
        P(rows, None),
    )
    out_specs = (
        P(rows, None),
        P(rows, None),
        P(rows, None),
        P(expert, None, "dp"),
        P(expert, None, "dp"),
    )
    return jax.shard_map(shards, mesh=fine, in_specs=in_specs, out_specs=out_specs, check_vma=False)
```

```python
import jax
import jax.numpy as jnp
from jax import lax
from jax.experimental import pallas as pl
from jax.experimental.pallas import tpu as pltpu
from jax.sharding import Mesh
from jax.sharding import PartitionSpec as P

GMAX = 3
SLOTS = 4
BF = jnp.bfloat16
F32 = jnp.float32


def merge_kernel(index_ref, coef_ref, rows_ref, out_ref):
    groups = out_ref.shape[0]

    def one(g, carry):
        total = coef_ref[GMAX * g] * rows_ref[index_ref[GMAX * g]].astype(F32)
        for m in range(1, GMAX):
            total = total + coef_ref[GMAX * g + m] * rows_ref[index_ref[GMAX * g + m]].astype(F32)
        out_ref[g] = total.astype(BF)
        return carry

    lax.fori_loop(0, groups, one, 0, unroll=4)


def merge(index_table, coef_table, rows):
    groups = index_table.shape[0]
    shape = (groups,) + rows.shape[1:]
    return pl.pallas_call(
        merge_kernel,
        out_shape=jax.ShapeDtypeStruct(shape, BF),
        in_specs=[
            pl.BlockSpec(memory_space=pltpu.SMEM),
            pl.BlockSpec(memory_space=pltpu.SMEM),
            pl.BlockSpec(memory_space=pltpu.VMEM),
        ],
        out_specs=pl.BlockSpec(memory_space=pltpu.VMEM),
        compiler_params=pltpu.CompilerParams(vmem_limit_bytes=24 * 2**20),
        cost_estimate=pl.CostEstimate(
            flops=0, bytes_accessed=2 * rows.size + 2 * groups * rows[0].size, transcendentals=0
        ),
    )(index_table.reshape(-1), coef_table.reshape(-1), rows)


def expert_kernel(rows_ref, up_ref, down_ref, out_ref, act_ref, hid_ref):
    rows = rows_ref[...]
    count = rows.shape[0]
    preact = jnp.dot(rows, up_ref[...], preferred_element_type=F32)
    hidden_grad = jnp.dot(rows, down_ref[...], preferred_element_type=F32)
    is_x = lax.broadcasted_iota(jnp.int32, preact.shape, 0) % (2 * SLOTS) < SLOTS
    sig = jax.nn.sigmoid(preact)
    slope = sig * (1.0 + preact * (1.0 - sig))
    hidden = jnp.where(is_x, preact * sig, 0.0)
    act_grad = jnp.where(is_x, pltpu.roll(hidden_grad, count - SLOTS, 0) * slope, 0.0)
    last = (((1,), (1,)), ((), ()))
    result = lax.dot_general(hidden.astype(BF), down_ref[...], last, preferred_element_type=F32)
    act_at_g = pltpu.roll(act_grad, SLOTS, 0).astype(BF)
    result = result + lax.dot_general(act_at_g, up_ref[...], last, preferred_element_type=F32)
    out_ref[...] = result.astype(BF)
    act_ref[...] = act_grad.T.astype(BF)
    hid_ref[...] = pltpu.roll(hidden, SLOTS, 0).T.astype(BF)


def expert(rows, w_up, w_down):
    count, width = rows.shape
    units = w_up.shape[1]
    tile = 256
    whole = pl.BlockSpec((width, units), lambda i: (0, 0))
    return pl.pallas_call(
        expert_kernel,
        grid=(count // tile,),
        out_shape=(
            jax.ShapeDtypeStruct((count, width), BF),
            jax.ShapeDtypeStruct((units, count), BF),
            jax.ShapeDtypeStruct((units, count), BF),
        ),
        in_specs=[pl.BlockSpec((tile, width), lambda i: (i, 0)), whole, whole],
        out_specs=(
            pl.BlockSpec((tile, width), lambda i: (i, 0)),
            pl.BlockSpec((units, tile), lambda i: (0, i)),
            pl.BlockSpec((units, tile), lambda i: (0, i)),
        ),
        compiler_params=pltpu.CompilerParams(vmem_limit_bytes=32 * 2**20),
        cost_estimate=pl.CostEstimate(
            flops=8 * count * width * units,
            bytes_accessed=4 * count * width + 4 * width * units + 4 * units * count,
            transcendentals=count * units,
        ),
    )(rows, w_up, w_down)


def shards(old_up, old_down, group_ids, freq_counts, tokens, routing, probs, cotangent):
    chips = lax.axis_size("chip")
    groups = chips
    width = tokens.shape[1]
    token_rows, chosen = routing.shape
    block = width // chips
    quarter = old_up.shape[3]
    both = ("chip", "core")

    member = (group_ids[None, :] == jnp.arange(groups, dtype=jnp.int32)[:, None]).astype(jnp.int32)
    rank = jnp.sum((jnp.cumsum(member, axis=1) - member) * member, axis=0)
    weights = freq_counts.astype(F32)
    totals = jnp.sum(member.astype(F32) * weights[None, :], axis=1)
    merge_coef = member.astype(F32) * weights[None, :] / totals[:, None]
    select = member[:, None, :] * (
        rank[None, None, :] == jnp.arange(GMAX, dtype=jnp.int32)[None, :, None]
    ).astype(jnp.int32)
    index_table = jnp.sum(
        select * jnp.arange(member.shape[1], dtype=jnp.int32)[None, None, :], axis=2
    ).astype(jnp.int32)
    coef_table = jnp.sum(select.astype(F32) * merge_coef[:, None, :], axis=2)

    def by_owner(w):
        return w.reshape(chips, block, 2, quarter).transpose(0, 2, 1, 3)

    spread = jnp.concatenate([by_owner(old_up), by_owner(old_down)], axis=2)
    spread = spread.reshape(2 * chips, 2 * block, quarter)
    spread = lax.all_to_all(spread, both, split_axis=0, concat_axis=0, tiled=True)
    merged = merge(index_table, coef_table, spread)
    merged = lax.all_to_all(merged, "chip", split_axis=0, concat_axis=0, tiled=True)
    up_half = merged[:, :block].reshape(width, quarter)
    down_half = merged[:, block:].reshape(width, quarter)
    w_up = lax.all_gather(up_half, "dp", axis=1, tiled=True)
    w_down = lax.all_gather(down_half, "dp", axis=1, tiled=True)

    flat = routing.reshape(-1)
    onehot = (flat[:, None] == jnp.arange(groups, dtype=jnp.int32)[None, :]).astype(jnp.int32)
    order_rank = jnp.sum((jnp.cumsum(onehot, axis=0) - onehot) * onehot, axis=1)
    slot_of = (flat * (2 * SLOTS) + order_rank).reshape(token_rows, chosen)
    places = groups * 2 * SLOTS
    place = jnp.arange(places, dtype=jnp.int32)
    hit_x = place[:, None, None] == slot_of[None]
    hit_g = place[:, None, None] == slot_of[None] + SLOTS
    map_x = jnp.any(hit_x, axis=2).astype(BF)
    map_g = jnp.any(hit_g, axis=2).astype(BF)
    row_p = jnp.sum(jnp.where(hit_g, probs[None], 0.0), axis=(1, 2))
    factor = jnp.where((place // SLOTS) % 2 == 0, 1.0, row_p)
    pick = jnp.concatenate([map_x, map_g], axis=1)
    both_rows = jnp.concatenate([tokens, cotangent], axis=0)
    send = (jnp.dot(pick, both_rows, preferred_element_type=F32) * factor[:, None]).astype(BF)
    send = send.reshape(groups, 2 * SLOTS, width)
    send, merged = lax.optimization_barrier((send, merged))
    recv = lax.all_to_all(send, "chip", split_axis=0, concat_axis=0, tiled=True)
    swap = [(0, 1), (1, 0)]
    per = chips * 2 * SLOTS
    recv = recv.reshape(per, width)
    other = lax.ppermute(recv, "core", swap)

    mine, act_mine, hid_mine = expert(recv, w_up, w_down)
    theirs, act_theirs, hid_theirs = expert(other, w_up, w_down)
    arrived = lax.ppermute(theirs, "core", swap)
    back = (mine.astype(F32) + arrived.astype(F32)).astype(BF).reshape(groups, 2 * SLOTS, width)
    back = lax.all_to_all(back, "chip", split_axis=0, concat_axis=0, tiled=True)
    back = back.reshape(places, width)

    def weight_grad(left_mine, left_theirs):
        part = jnp.dot(left_mine, recv, preferred_element_type=F32)
        part = part + jnp.dot(left_theirs, other, preferred_element_type=F32)
        return lax.psum_scatter(part.astype(BF), "dp", scatter_dimension=0, tiled=True).T

    up_share = weight_grad(act_mine, act_theirs)
    down_share = weight_grad(hid_mine, hid_theirs)

    with_p = jnp.sum(jnp.where(hit_x, probs[None], 0.0), axis=2).T
    p_high = with_p.astype(BF)
    p_low = (with_p - p_high.astype(F32)).astype(BF)
    gather = jnp.concatenate([p_high, p_low, map_g.T], axis=0)
    last = (((1,), (1,)), ((), ()))
    sums = jnp.dot(gather, back, preferred_element_type=F32)
    layer_out = (sums[:token_rows] + sums[token_rows : 2 * token_rows]).astype(BF)
    token_grad = sums[2 * token_rows :].astype(BF)
    gates = lax.dot_general(cotangent, back, last, preferred_element_type=F32)
    gate_grad = jnp.sum(
        jnp.where(slot_of[:, :, None] == place[None, None, :], gates[:, None, :], 0.0), axis=2
    )
    return layer_out, token_grad, gate_grad, up_share[None], down_share[None]


def solution(mesh):
    experts, data = mesh.devices.shape
    fine = Mesh(mesh.devices.reshape(experts // 2, 2, data), ("chip", "core", "dp"))
    expert = ("chip", "core")
    rows = ("chip", "core", "dp")
    in_specs = (
        P(expert, None, None, "dp"),
        P(expert, None, None, "dp"),
        P(),
        P(),
        P(rows, None),
        P(rows, None),
        P(rows, None),
        P(rows, None),
    )
    out_specs = (
        P(rows, None),
        P(rows, None),
        P(rows, None),
        P(expert, None, "dp"),
        P(expert, None, "dp"),
    )
    return jax.shard_map(shards, mesh=fine, in_specs=in_specs, out_specs=out_specs, check_vma=False)
```

```python
import jax
import jax.numpy as jnp
from jax import lax
from jax.experimental import pallas as pl
from jax.experimental.pallas import tpu as pltpu
from jax.sharding import Mesh
from jax.sharding import PartitionSpec as P

GMAX = 3
LANES = 128
SLOTS = 4
BF = jnp.bfloat16
F32 = jnp.float32


def merge_kernel(index_ref, coef_ref, rows_ref, up_ref, down_ref):
    groups, block = up_ref.shape[:2]

    def one(g, carry):
        total = coef_ref[GMAX * g] * rows_ref[index_ref[GMAX * g]].astype(F32)
        for m in range(1, GMAX):
            total = total + coef_ref[GMAX * g + m] * rows_ref[index_ref[GMAX * g + m]].astype(F32)
        merged = total.astype(BF)
        up_ref[g] = merged[:block]
        down_ref[g] = merged[block:]
        return carry

    lax.fori_loop(0, groups, one, 0, unroll=4)


def merge(index_table, coef_table, rows):
    groups = index_table.shape[0]
    half = jax.ShapeDtypeStruct((groups, rows.shape[1] // 2, rows.shape[2]), BF)
    vmem = pl.BlockSpec(memory_space=pltpu.VMEM)
    return pl.pallas_call(
        merge_kernel,
        out_shape=(half, half),
        in_specs=[
            pl.BlockSpec(memory_space=pltpu.SMEM),
            pl.BlockSpec(memory_space=pltpu.SMEM),
            vmem,
        ],
        out_specs=(vmem, vmem),
        compiler_params=pltpu.CompilerParams(vmem_limit_bytes=24 * 2**20),
        cost_estimate=pl.CostEstimate(
            flops=0, bytes_accessed=2 * rows.size + 4 * half.size, transcendentals=0
        ),
    )(index_table.reshape(-1), coef_table.reshape(-1), rows)


def expert_kernel(rows_ref, up_ref, down_ref, out_ref, act_ref, hid_ref):
    rows = rows_ref[...]
    count = rows.shape[0]
    preact = jnp.dot(rows, up_ref[...], preferred_element_type=F32)
    hidden_grad = jnp.dot(rows, down_ref[...], preferred_element_type=F32)
    is_x = lax.broadcasted_iota(jnp.int32, preact.shape, 0) % (2 * SLOTS) < SLOTS
    sig = jax.nn.sigmoid(preact)
    slope = sig * (1.0 + preact * (1.0 - sig))
    hidden = jnp.where(is_x, preact * sig, 0.0)
    act_grad = jnp.where(is_x, pltpu.roll(hidden_grad, count - SLOTS, 0) * slope, 0.0)
    last = (((1,), (1,)), ((), ()))
    result = lax.dot_general(hidden.astype(BF), down_ref[...], last, preferred_element_type=F32)
    act_at_g = pltpu.roll(act_grad, SLOTS, 0).astype(BF)
    result = result + lax.dot_general(act_at_g, up_ref[...], last, preferred_element_type=F32)
    out_ref[...] = result.astype(BF)
    act_ref[...] = act_grad.T.astype(BF)
    hid_ref[...] = pltpu.roll(hidden, SLOTS, 0).T.astype(BF)


def expert(rows, w_up, w_down):
    count, width = rows.shape
    units = w_up.shape[1]
    tile = 256
    whole = pl.BlockSpec((width, units), lambda i: (0, 0))
    return pl.pallas_call(
        expert_kernel,
        grid=(count // tile,),
        out_shape=(
            jax.ShapeDtypeStruct((count, width), BF),
            jax.ShapeDtypeStruct((units, count), BF),
            jax.ShapeDtypeStruct((units, count), BF),
        ),
        in_specs=[pl.BlockSpec((tile, width), lambda i: (i, 0)), whole, whole],
        out_specs=(
            pl.BlockSpec((tile, width), lambda i: (i, 0)),
            pl.BlockSpec((units, tile), lambda i: (0, i)),
            pl.BlockSpec((units, tile), lambda i: (0, i)),
        ),
        compiler_params=pltpu.CompilerParams(vmem_limit_bytes=32 * 2**20),
        cost_estimate=pl.CostEstimate(
            flops=8 * count * width * units,
            bytes_accessed=4 * count * width + 4 * width * units + 4 * units * count,
            transcendentals=count * units,
        ),
    )(rows, w_up, w_down)


def shards(old_up, old_down, group_ids, freq_counts, tokens, routing, probs, cotangent):
    columns, depth = lax.axis_size("y"), lax.axis_size("z")
    chips = columns * depth
    groups = chips
    width = tokens.shape[1]
    token_rows, chosen = routing.shape
    block = width // chips
    quarter = old_up.shape[3]
    chip = ("y", "z")
    both = ("y", "z", "core")

    member = (group_ids[None, :] == jnp.arange(groups, dtype=jnp.int32)[:, None]).astype(jnp.int32)
    rank = jnp.sum((jnp.cumsum(member, axis=1) - member) * member, axis=0)
    weights = freq_counts.astype(F32)
    totals = jnp.sum(member.astype(F32) * weights[None, :], axis=1)
    merge_coef = member.astype(F32) * weights[None, :] / totals[:, None]
    select = member[:, None, :] * (
        rank[None, None, :] == jnp.arange(GMAX, dtype=jnp.int32)[None, :, None]
    ).astype(jnp.int32)
    index_table = jnp.sum(
        select * jnp.arange(member.shape[1], dtype=jnp.int32)[None, None, :], axis=2
    ).astype(jnp.int32)
    coef_table = jnp.sum(select.astype(F32) * merge_coef[:, None, :], axis=2)

    def by_owner(w):
        return w.reshape(chips, block, 2, quarter).transpose(0, 2, 1, 3)

    spread = jnp.concatenate([by_owner(old_up), by_owner(old_down)], axis=2)
    spread = spread.reshape(2 * chips, 2 * block, quarter)
    spread = lax.all_to_all(spread, both, split_axis=0, concat_axis=0, tiled=True)
    up_half, down_half = merge(index_table, coef_table, spread)
    up_half = lax.all_to_all(up_half, chip, split_axis=0, concat_axis=0, tiled=True)
    down_half, up_half = lax.optimization_barrier((down_half, up_half))
    w_up = lax.all_gather(up_half.reshape(width, quarter), "dp", axis=1, tiled=True)
    down_half = lax.all_to_all(down_half, chip, split_axis=0, concat_axis=0, tiled=True)
    w_down = lax.all_gather(down_half.reshape(width, quarter), "dp", axis=1, tiled=True)

    p_high = probs.astype(BF)
    p_rest = probs - p_high.astype(F32)
    p_mid = p_rest.astype(BF)
    p_low = (p_rest - p_mid.astype(F32)).astype(BF)
    notes = jnp.concatenate([routing.astype(BF), p_high, p_mid, p_low], axis=1)
    notes = jnp.pad(notes, ((0, 0), (0, LANES - notes.shape[1])))
    packed = jnp.concatenate([tokens, cotangent, notes], axis=1)
    column = lax.all_gather(packed, "z", axis=0, tiled=True)
    col_tokens = column[:, :width]
    col_cot = column[:, width : 2 * width]
    col_notes = column[:, 2 * width :].astype(F32)
    col_routing = col_notes[:, :chosen].astype(jnp.int32)
    col_p = col_notes[:, chosen : 2 * chosen] + col_notes[:, 2 * chosen : 3 * chosen]
    col_p = col_p + col_notes[:, 3 * chosen : 4 * chosen]

    count = depth * token_rows
    experts = jnp.arange(columns, dtype=jnp.int32) * depth + lax.axis_index("z")
    named = col_routing[None] == experts[:, None, None]
    names = jnp.any(named, axis=2).astype(jnp.int32)
    weight = jnp.sum(jnp.where(named, col_p[None], 0.0), axis=2)
    inside = names.reshape(columns, depth, token_rows)
    order = (jnp.cumsum(inside, axis=2) - inside).reshape(columns, count)
    source = jnp.arange(count, dtype=jnp.int32)[None, :] // token_rows
    row_at = (jnp.arange(columns, dtype=jnp.int32)[:, None] * depth + source) * (2 * SLOTS) + order
    row_at = jnp.where(names > 0, row_at, -2 * SLOTS)
    sent = columns * depth * 2 * SLOTS
    row_id = jnp.arange(sent, dtype=jnp.int32)
    hit_tok = row_id[:, None, None] == row_at[None]
    hit_cot = row_id[:, None, None] == row_at[None] + SLOTS
    pick = jnp.concatenate([jnp.any(hit_tok, axis=1), jnp.any(hit_cot, axis=1)], axis=1).astype(BF)
    row_p = jnp.sum(jnp.where(hit_cot, weight[None], 0.0), axis=(1, 2))
    factor = jnp.where((row_id // SLOTS) % 2 == 0, 1.0, row_p)
    send = jnp.dot(pick[:, :count], col_tokens, preferred_element_type=F32)
    send = send + jnp.dot(pick[:, count:], col_cot, preferred_element_type=F32)
    send = (send * factor[:, None]).astype(BF).reshape(columns, depth * 2 * SLOTS, width)
    send, down_half = lax.optimization_barrier((send, down_half))
    recv = lax.all_to_all(send, "y", split_axis=0, concat_axis=0, tiled=True)

    flat = routing.reshape(-1)
    onehot = (flat[:, None] == jnp.arange(groups, dtype=jnp.int32)[None, :]).astype(jnp.int32)
    order_rank = jnp.sum((jnp.cumsum(onehot, axis=0) - onehot) * onehot, axis=1)
    slot_of = (flat * (2 * SLOTS) + order_rank).reshape(token_rows, chosen)
    places = groups * 2 * SLOTS
    place = jnp.arange(places, dtype=jnp.int32)
    hit_x = place[:, None, None] == slot_of[None]
    hit_g = place[:, None, None] == slot_of[None] + SLOTS
    map_g = jnp.any(hit_g, axis=2).astype(BF)
    swap = [(0, 1), (1, 0)]
    per = chips * 2 * SLOTS
    recv = recv.reshape(per, width)
    other = lax.ppermute(recv, "core", swap)

    mine, act_mine, hid_mine = expert(recv, w_up, w_down)
    theirs, act_theirs, hid_theirs = expert(other, w_up, w_down)
    arrived = lax.ppermute(theirs, "core", swap)
    back = (mine.astype(F32) + arrived.astype(F32)).astype(BF).reshape(groups, 2 * SLOTS, width)
    back = lax.all_to_all(back, chip, split_axis=0, concat_axis=0, tiled=True)
    back = back.reshape(places, width)

    def weight_grad(left_mine, left_theirs):
        part = jnp.dot(left_mine, recv, preferred_element_type=F32)
        part = part + jnp.dot(left_theirs, other, preferred_element_type=F32)
        return lax.psum_scatter(part.astype(BF), "dp", scatter_dimension=0, tiled=True).T

    up_share = weight_grad(act_mine, act_theirs)
    down_share = weight_grad(hid_mine, hid_theirs)

    with_p = jnp.sum(jnp.where(hit_x, probs[None], 0.0), axis=2).T
    p_high = with_p.astype(BF)
    p_low = (with_p - p_high.astype(F32)).astype(BF)
    gather = jnp.concatenate([p_high, p_low, map_g.T], axis=0)
    last = (((1,), (1,)), ((), ()))
    sums = jnp.dot(gather, back, preferred_element_type=F32)
    layer_out = (sums[:token_rows] + sums[token_rows : 2 * token_rows]).astype(BF)
    token_grad = sums[2 * token_rows :].astype(BF)
    gates = lax.dot_general(cotangent, back, last, preferred_element_type=F32)
    gate_grad = jnp.sum(
        jnp.where(slot_of[:, :, None] == place[None, None, :], gates[:, None, :], 0.0), axis=2
    )
    return layer_out, token_grad, gate_grad, up_share[None], down_share[None]


def solution(mesh):
    experts, data = mesh.devices.shape
    columns = data
    depth = experts // (2 * columns)
    fine = Mesh(mesh.devices.reshape(columns, depth, 2, data), ("y", "z", "core", "dp"))
    expert = ("y", "z", "core")
    rows = ("y", "z", "core", "dp")
    in_specs = (
        P(expert, None, None, "dp"),
        P(expert, None, None, "dp"),
        P(),
        P(),
        P(rows, None),
        P(rows, None),
        P(rows, None),
        P(rows, None),
    )
    out_specs = (
        P(rows, None),
        P(rows, None),
        P(rows, None),
        P(expert, None, "dp"),
        P(expert, None, "dp"),
    )
    return jax.shard_map(shards, mesh=fine, in_specs=in_specs, out_specs=out_specs, check_vma=False)
```

```python
import jax
import jax.numpy as jnp
from jax import lax
from jax.experimental import pallas as pl
from jax.experimental.pallas import tpu as pltpu
from jax.sharding import Mesh
from jax.sharding import PartitionSpec as P

GMAX = 3
LANES = 128
SLOTS = 4
BF = jnp.bfloat16
F32 = jnp.float32


def merge_kernel(index_ref, coef_ref, rows_ref, up_ref, down_ref):
    groups, block = up_ref.shape[:2]

    def one(g, carry):
        total = coef_ref[GMAX * g] * rows_ref[index_ref[GMAX * g]].astype(F32)
        for m in range(1, GMAX):
            total = total + coef_ref[GMAX * g + m] * rows_ref[index_ref[GMAX * g + m]].astype(F32)
        merged = total.astype(BF)
        up_ref[g] = merged[:block]
        down_ref[g] = merged[block:]
        return carry

    lax.fori_loop(0, groups, one, 0, unroll=4)


def merge(index_table, coef_table, rows):
    groups = index_table.shape[0]
    half = jax.ShapeDtypeStruct((groups, rows.shape[1] // 2, rows.shape[2]), BF)
    vmem = pl.BlockSpec(memory_space=pltpu.VMEM)
    return pl.pallas_call(
        merge_kernel,
        out_shape=(half, half),
        in_specs=[
            pl.BlockSpec(memory_space=pltpu.SMEM),
            pl.BlockSpec(memory_space=pltpu.SMEM),
            vmem,
        ],
        out_specs=(vmem, vmem),
        compiler_params=pltpu.CompilerParams(vmem_limit_bytes=24 * 2**20),
        cost_estimate=pl.CostEstimate(
            flops=0, bytes_accessed=2 * rows.size + 4 * half.size, transcendentals=0
        ),
    )(index_table.reshape(-1), coef_table.reshape(-1), rows)


VMEM = pl.BlockSpec(memory_space=pltpu.VMEM)
TILE = 256
LAST = (((1,), (1,)), ((), ()))


def hidden_kernel(rows_ref, up_ref, hid_ref, slope_ref, hid_t_ref):
    for start in range(0, rows_ref.shape[0], TILE):
        at = pl.ds(start, TILE)
        preact = jnp.dot(rows_ref[at], up_ref[...], preferred_element_type=F32)
        is_x = lax.broadcasted_iota(jnp.int32, preact.shape, 0) % (2 * SLOTS) < SLOTS
        sig = jax.nn.sigmoid(preact)
        hidden = jnp.where(is_x, preact * sig, 0.0)
        hid_ref[at] = hidden.astype(BF)
        slope_ref[at] = jnp.where(is_x, sig * (1.0 + preact * (1.0 - sig)), 0.0)
        hid_t_ref[:, at] = pltpu.roll(hidden, SLOTS, 0).T.astype(BF)


def hidden_rows(rows, w_up):
    count, width = rows.shape
    units = w_up.shape[1]
    return pl.pallas_call(
        hidden_kernel,
        out_shape=(
            jax.ShapeDtypeStruct((count, units), BF),
            jax.ShapeDtypeStruct((count, units), F32),
            jax.ShapeDtypeStruct((units, count), BF),
        ),
        in_specs=[VMEM] * 2,
        out_specs=(VMEM,) * 3,
        compiler_params=pltpu.CompilerParams(vmem_limit_bytes=32 * 2**20),
        cost_estimate=pl.CostEstimate(
            flops=2 * count * width * units,
            bytes_accessed=2 * count * width + 2 * width * units + 8 * units * count,
            transcendentals=count * units,
        ),
    )(rows, w_up)


def expert_kernel(rows_ref, hid_ref, slope_ref, up_ref, down_ref, out_ref, act_t_ref):
    for start in range(0, rows_ref.shape[0], TILE):
        at = pl.ds(start, TILE)
        hidden_grad = jnp.dot(rows_ref[at], down_ref[...], preferred_element_type=F32)
        act_grad = pltpu.roll(hidden_grad, TILE - SLOTS, 0) * slope_ref[at]
        act_at_g = pltpu.roll(act_grad, SLOTS, 0).astype(BF)
        result = lax.dot_general(hid_ref[at], down_ref[...], LAST, preferred_element_type=F32)
        result = result + lax.dot_general(act_at_g, up_ref[...], LAST, preferred_element_type=F32)
        out_ref[at] = result.astype(BF)
        act_t_ref[:, at] = act_grad.T.astype(BF)


def expert(rows, hidden, slope, w_up, w_down):
    count, width = rows.shape
    units = w_up.shape[1]
    return pl.pallas_call(
        expert_kernel,
        out_shape=(
            jax.ShapeDtypeStruct((count, width), BF),
            jax.ShapeDtypeStruct((units, count), BF),
        ),
        in_specs=[VMEM] * 5,
        out_specs=(VMEM,) * 2,
        compiler_params=pltpu.CompilerParams(vmem_limit_bytes=40 * 2**20),
        cost_estimate=pl.CostEstimate(
            flops=6 * count * width * units,
            bytes_accessed=4 * count * width + 4 * width * units + 8 * units * count,
            transcendentals=0,
        ),
    )(rows, hidden, slope, w_up, w_down)


def grad_kernel(mine_ref, theirs_ref, recv_ref, other_ref, out_ref):
    for start in range(0, recv_ref.shape[1], 2 * TILE):
        at = pl.ds(start, 2 * TILE)
        part = jnp.dot(mine_ref[...], recv_ref[:, at], preferred_element_type=F32)
        part = part + jnp.dot(theirs_ref[...], other_ref[:, at], preferred_element_type=F32)
        out_ref[:, at] = part.astype(BF)


def weight_part(left_mine, left_theirs, recv, other):
    units, count = left_mine.shape
    width = recv.shape[1]
    return pl.pallas_call(
        grad_kernel,
        out_shape=jax.ShapeDtypeStruct((units, width), BF),
        in_specs=[VMEM] * 4,
        out_specs=VMEM,
        compiler_params=pltpu.CompilerParams(vmem_limit_bytes=32 * 2**20),
        cost_estimate=pl.CostEstimate(
            flops=4 * count * width * units,
            bytes_accessed=4 * count * width + 4 * units * count + 2 * units * width,
            transcendentals=0,
        ),
    )(left_mine, left_theirs, recv, other)


def over_dp(part):
    return lax.psum_scatter(part, "dp", scatter_dimension=0, tiled=True).T


def combine_kernel(pick_ref, back_ref, cot_ref, slot_ref, layer_ref, token_ref, gate_ref):
    tokens, chosen = slot_ref.shape
    back = back_ref[...]
    sums = jnp.dot(pick_ref[...], back, preferred_element_type=F32)
    layer_ref[...] = (sums[:tokens] + sums[tokens : 2 * tokens]).astype(BF)
    token_ref[...] = sums[2 * tokens :].astype(BF)
    gates = lax.dot_general(cot_ref[...], back, LAST, preferred_element_type=F32)
    place = lax.broadcasted_iota(jnp.int32, gates.shape, 1)
    column = lax.broadcasted_iota(jnp.int32, (tokens, chosen), 1)
    gate = jnp.zeros((tokens, chosen), F32)
    for k in range(chosen):
        found = jnp.where(place == slot_ref[:, k : k + 1], gates, 0.0)
        gate = jnp.where(column == k, jnp.sum(found, axis=1, keepdims=True), gate)
    gate_ref[...] = gate


def combine(pick, back, cotangent, slot_of):
    shape = jax.ShapeDtypeStruct(cotangent.shape, BF)
    return pl.pallas_call(
        combine_kernel,
        out_shape=(shape, shape, jax.ShapeDtypeStruct(slot_of.shape, F32)),
        in_specs=[VMEM] * 4,
        out_specs=(VMEM,) * 3,
        compiler_params=pltpu.CompilerParams(vmem_limit_bytes=16 * 2**20),
        cost_estimate=pl.CostEstimate(
            flops=128 * back.size, bytes_accessed=2 * back.size, transcendentals=0
        ),
    )(pick, back, cotangent, slot_of)


def shards(old_up, old_down, group_ids, freq_counts, tokens, routing, probs, cotangent):
    columns, depth = lax.axis_size("y"), lax.axis_size("z")
    chips = columns * depth
    groups = chips
    width = tokens.shape[1]
    token_rows, chosen = routing.shape
    block = width // chips
    quarter = old_up.shape[3]
    chip = ("y", "z")
    both = ("y", "z", "core")

    member = (group_ids[None, :] == jnp.arange(groups, dtype=jnp.int32)[:, None]).astype(jnp.int32)
    rank = jnp.sum((jnp.cumsum(member, axis=1) - member) * member, axis=0)
    weights = freq_counts.astype(F32)
    totals = jnp.sum(member.astype(F32) * weights[None, :], axis=1)
    merge_coef = member.astype(F32) * weights[None, :] / totals[:, None]
    select = member[:, None, :] * (
        rank[None, None, :] == jnp.arange(GMAX, dtype=jnp.int32)[None, :, None]
    ).astype(jnp.int32)
    index_table = jnp.sum(
        select * jnp.arange(member.shape[1], dtype=jnp.int32)[None, None, :], axis=2
    ).astype(jnp.int32)
    coef_table = jnp.sum(select.astype(F32) * merge_coef[:, None, :], axis=2)

    def by_owner(w):
        return w.reshape(chips, block, 2, quarter).transpose(0, 2, 1, 3)

    spread = jnp.concatenate([by_owner(old_up), by_owner(old_down)], axis=2)
    spread = spread.reshape(2 * chips, 2 * block, quarter)
    spread = lax.all_to_all(spread, both, split_axis=0, concat_axis=0, tiled=True)
    up_half, down_half = merge(index_table, coef_table, spread)
    up_half = lax.all_to_all(up_half, chip, split_axis=0, concat_axis=0, tiled=True)
    down_half, up_half = lax.optimization_barrier((down_half, up_half))
    w_up = lax.all_gather(up_half.reshape(width, quarter), "dp", axis=1, tiled=True)
    down_half = lax.all_to_all(down_half, chip, split_axis=0, concat_axis=0, tiled=True)
    w_down = lax.all_gather(down_half.reshape(width, quarter), "dp", axis=1, tiled=True)

    p_high = probs.astype(BF)
    p_rest = probs - p_high.astype(F32)
    p_mid = p_rest.astype(BF)
    p_low = (p_rest - p_mid.astype(F32)).astype(BF)
    notes = jnp.concatenate([routing.astype(BF), p_high, p_mid, p_low], axis=1)
    notes = jnp.pad(notes, ((0, 0), (0, LANES - notes.shape[1])))
    packed = jnp.concatenate([tokens, cotangent, notes], axis=1)
    column = lax.all_gather(packed, "z", axis=0, tiled=True)
    col_tokens = column[:, :width]
    col_cot = column[:, width : 2 * width]
    col_notes = column[:, 2 * width :].astype(F32)
    col_routing = col_notes[:, :chosen].astype(jnp.int32)
    col_p = col_notes[:, chosen : 2 * chosen] + col_notes[:, 2 * chosen : 3 * chosen]
    col_p = col_p + col_notes[:, 3 * chosen : 4 * chosen]

    count = depth * token_rows
    experts = jnp.arange(columns, dtype=jnp.int32) * depth + lax.axis_index("z")
    named = col_routing[None] == experts[:, None, None]
    names = jnp.any(named, axis=2).astype(jnp.int32)
    weight = jnp.sum(jnp.where(named, col_p[None], 0.0), axis=2)
    inside = names.reshape(columns, depth, token_rows)
    order = (jnp.cumsum(inside, axis=2) - inside).reshape(columns, count)
    source = jnp.arange(count, dtype=jnp.int32)[None, :] // token_rows
    row_at = (jnp.arange(columns, dtype=jnp.int32)[:, None] * depth + source) * (2 * SLOTS) + order
    row_at = jnp.where(names > 0, row_at, -2 * SLOTS)
    sent = columns * depth * 2 * SLOTS
    row_id = jnp.arange(sent, dtype=jnp.int32)
    hit_tok = row_id[:, None, None] == row_at[None]
    hit_cot = row_id[:, None, None] == row_at[None] + SLOTS
    pick = jnp.concatenate([jnp.any(hit_tok, axis=1), jnp.any(hit_cot, axis=1)], axis=1).astype(BF)
    row_p = jnp.sum(jnp.where(hit_cot, weight[None], 0.0), axis=(1, 2))
    factor = jnp.where((row_id // SLOTS) % 2 == 0, 1.0, row_p)
    send = jnp.dot(pick[:, :count], col_tokens, preferred_element_type=F32)
    send = send + jnp.dot(pick[:, count:], col_cot, preferred_element_type=F32)
    send, factor, down_half = lax.optimization_barrier((send, factor, down_half))
    send = (send * factor[:, None]).astype(BF).reshape(columns, depth * 2 * SLOTS, width)
    recv = lax.all_to_all(send, "y", split_axis=0, concat_axis=0, tiled=True)

    flat = routing.reshape(-1)
    onehot = (flat[:, None] == jnp.arange(groups, dtype=jnp.int32)[None, :]).astype(jnp.int32)
    order_rank = jnp.sum((jnp.cumsum(onehot, axis=0) - onehot) * onehot, axis=1)
    slot_of = (flat * (2 * SLOTS) + order_rank).reshape(token_rows, chosen)
    places = groups * 2 * SLOTS
    place = jnp.arange(places, dtype=jnp.int32)
    hit_x = place[:, None, None] == slot_of[None]
    hit_g = place[:, None, None] == slot_of[None] + SLOTS
    map_g = jnp.any(hit_g, axis=2).astype(BF)
    swap = [(0, 1), (1, 0)]
    per = chips * 2 * SLOTS
    recv = recv.reshape(per, width)
    other = lax.ppermute(recv, "core", swap)

    hid_mine, slope_mine, hid_t_mine = hidden_rows(recv, w_up)
    hid_theirs, slope_theirs, hid_t_theirs = hidden_rows(other, w_up)
    down_part = weight_part(hid_t_mine, hid_t_theirs, recv, other)
    w_down, hid_mine, hid_theirs, down_part = lax.optimization_barrier(
        (w_down, hid_mine, hid_theirs, down_part)
    )
    down_share = over_dp(down_part)
    theirs, act_t_theirs = expert(other, hid_theirs, slope_theirs, w_up, w_down)
    arrived = lax.ppermute(theirs, "core", swap)
    mine, act_t_mine = expert(recv, hid_mine, slope_mine, w_up, w_down)
    back, act_t_mine = lax.optimization_barrier((mine + arrived, act_t_mine))
    back = back.reshape(groups, 2 * SLOTS, width)
    back = lax.all_to_all(back, chip, split_axis=0, concat_axis=0, tiled=True)
    back = back.reshape(places, width)
    up_share = over_dp(weight_part(act_t_mine, act_t_theirs, recv, other))

    with_p = jnp.sum(jnp.where(hit_x, probs[None], 0.0), axis=2).T
    p_high = with_p.astype(BF)
    p_low = (with_p - p_high.astype(F32)).astype(BF)
    gather = jnp.concatenate([p_high, p_low, map_g.T], axis=0)
    layer_out, token_grad, gate_grad = combine(gather, back, cotangent, slot_of)
    return layer_out, token_grad, gate_grad, up_share[None], down_share[None]


def solution(mesh):
    experts, data = mesh.devices.shape
    columns = data
    depth = experts // (2 * columns)
    fine = Mesh(mesh.devices.reshape(columns, depth, 2, data), ("y", "z", "core", "dp"))
    expert = ("y", "z", "core")
    rows = ("y", "z", "core", "dp")
    in_specs = (
        P(expert, None, None, "dp"),
        P(expert, None, None, "dp"),
        P(),
        P(),
        P(rows, None),
        P(rows, None),
        P(rows, None),
        P(rows, None),
    )
    out_specs = (
        P(rows, None),
        P(rows, None),
        P(rows, None),
        P(expert, None, "dp"),
        P(expert, None, "dp"),
    )
    return jax.shard_map(shards, mesh=fine, in_specs=in_specs, out_specs=out_specs, check_vma=False)
```

```python
import jax
import jax.numpy as jnp
from jax import lax
from jax.experimental import pallas as pl
from jax.experimental.pallas import tpu as pltpu
from jax.sharding import Mesh
from jax.sharding import PartitionSpec as P

GMAX = 3
LANES = 128
SLOTS = 4
BF = jnp.bfloat16
F32 = jnp.float32


def merge_kernel(index_ref, coef_ref, rows_ref, up_ref, down_ref):
    groups, block = up_ref.shape[:2]

    def one(g, carry):
        total = coef_ref[GMAX * g] * rows_ref[index_ref[GMAX * g]].astype(F32)
        for m in range(1, GMAX):
            total = total + coef_ref[GMAX * g + m] * rows_ref[index_ref[GMAX * g + m]].astype(F32)
        merged = total.astype(BF)
        up_ref[g] = merged[:block]
        down_ref[g] = merged[block:]
        return carry

    lax.fori_loop(0, groups, one, 0, unroll=4)


def merge(index_table, coef_table, rows):
    groups = index_table.shape[0]
    half = jax.ShapeDtypeStruct((groups, rows.shape[1] // 2, rows.shape[2]), BF)
    vmem = pl.BlockSpec(memory_space=pltpu.VMEM)
    return pl.pallas_call(
        merge_kernel,
        out_shape=(half, half),
        in_specs=[
            pl.BlockSpec(memory_space=pltpu.SMEM),
            pl.BlockSpec(memory_space=pltpu.SMEM),
            vmem,
        ],
        out_specs=(vmem, vmem),
        compiler_params=pltpu.CompilerParams(vmem_limit_bytes=24 * 2**20),
        cost_estimate=pl.CostEstimate(
            flops=0, bytes_accessed=2 * rows.size + 4 * half.size, transcendentals=0
        ),
    )(index_table.reshape(-1), coef_table.reshape(-1), rows)


VMEM = pl.BlockSpec(memory_space=pltpu.VMEM)
TILE = 256
LAST = (((1,), (1,)), ((), ()))


def expert_kernel(rows_ref, up_ref, down_ref, out_ref, act_ref, hid_ref):
    rows = rows_ref[...]
    count = rows.shape[0]
    preact = jnp.dot(rows, up_ref[...], preferred_element_type=F32)
    hidden_grad = jnp.dot(rows, down_ref[...], preferred_element_type=F32)
    is_x = lax.broadcasted_iota(jnp.int32, preact.shape, 0) % (2 * SLOTS) < SLOTS
    sig = jax.nn.sigmoid(preact)
    slope = sig * (1.0 + preact * (1.0 - sig))
    hidden = jnp.where(is_x, preact * sig, 0.0)
    act_grad = jnp.where(is_x, pltpu.roll(hidden_grad, count - SLOTS, 0) * slope, 0.0)
    last = (((1,), (1,)), ((), ()))
    result = lax.dot_general(hidden.astype(BF), down_ref[...], last, preferred_element_type=F32)
    act_at_g = pltpu.roll(act_grad, SLOTS, 0).astype(BF)
    result = result + lax.dot_general(act_at_g, up_ref[...], last, preferred_element_type=F32)
    out_ref[...] = result.astype(BF)
    act_ref[...] = act_grad.T.astype(BF)
    hid_ref[...] = pltpu.roll(hidden, SLOTS, 0).T.astype(BF)


def expert(rows, w_up, w_down):
    count, width = rows.shape
    units = w_up.shape[1]
    tile = 256
    whole = pl.BlockSpec((width, units), lambda i: (0, 0))
    return pl.pallas_call(
        expert_kernel,
        grid=(count // tile,),
        out_shape=(
            jax.ShapeDtypeStruct((count, width), BF),
            jax.ShapeDtypeStruct((units, count), BF),
            jax.ShapeDtypeStruct((units, count), BF),
        ),
        in_specs=[pl.BlockSpec((tile, width), lambda i: (i, 0)), whole, whole],
        out_specs=(
            pl.BlockSpec((tile, width), lambda i: (i, 0)),
            pl.BlockSpec((units, tile), lambda i: (0, i)),
            pl.BlockSpec((units, tile), lambda i: (0, i)),
        ),
        compiler_params=pltpu.CompilerParams(vmem_limit_bytes=32 * 2**20),
        cost_estimate=pl.CostEstimate(
            flops=8 * count * width * units,
            bytes_accessed=4 * count * width + 4 * width * units + 4 * units * count,
            transcendentals=count * units,
        ),
    )(rows, w_up, w_down)


def add_kernel(mine_ref, theirs_ref, out_ref):
    out_ref[...] = (mine_ref[...].astype(F32) + theirs_ref[...].astype(F32)).astype(BF)


def add_rows(mine, theirs):
    return pl.pallas_call(
        add_kernel,
        out_shape=jax.ShapeDtypeStruct(mine.shape, BF),
        in_specs=[VMEM] * 2,
        out_specs=VMEM,
        compiler_params=pltpu.CompilerParams(vmem_limit_bytes=12 * 2**20),
        cost_estimate=pl.CostEstimate(
            flops=mine.size, bytes_accessed=6 * mine.size, transcendentals=0
        ),
    )(mine, theirs)


def grad_kernel(mine_ref, theirs_ref, recv_ref, other_ref, out_ref):
    for start in range(0, recv_ref.shape[1], 2 * TILE):
        at = pl.ds(start, 2 * TILE)
        part = jnp.dot(mine_ref[...], recv_ref[:, at], preferred_element_type=F32)
        part = part + jnp.dot(theirs_ref[...], other_ref[:, at], preferred_element_type=F32)
        out_ref[:, at] = part.astype(BF)


def weight_part(left_mine, left_theirs, recv, other):
    units, count = left_mine.shape
    width = recv.shape[1]
    return pl.pallas_call(
        grad_kernel,
        out_shape=jax.ShapeDtypeStruct((units, width), BF),
        in_specs=[VMEM] * 4,
        out_specs=VMEM,
        compiler_params=pltpu.CompilerParams(vmem_limit_bytes=12 * 2**20),
        cost_estimate=pl.CostEstimate(
            flops=4 * count * width * units,
            bytes_accessed=4 * count * width + 4 * units * count + 2 * units * width,
            transcendentals=0,
        ),
    )(left_mine, left_theirs, recv, other)


def over_dp(part):
    return lax.psum_scatter(part, "dp", scatter_dimension=0, tiled=True).T


def combine_kernel(pick_ref, back_ref, cot_ref, slot_ref, layer_ref, token_ref, gate_ref):
    tokens, chosen = slot_ref.shape
    back = back_ref[...]
    sums = jnp.dot(pick_ref[...], back, preferred_element_type=F32)
    layer_ref[...] = (sums[:tokens] + sums[tokens : 2 * tokens]).astype(BF)
    token_ref[...] = sums[2 * tokens :].astype(BF)
    gates = lax.dot_general(cot_ref[...], back, LAST, preferred_element_type=F32)
    place = lax.broadcasted_iota(jnp.int32, gates.shape, 1)
    column = lax.broadcasted_iota(jnp.int32, (tokens, chosen), 1)
    gate = jnp.zeros((tokens, chosen), F32)
    for k in range(chosen):
        found = jnp.where(place == slot_ref[:, k : k + 1], gates, 0.0)
        gate = jnp.where(column == k, jnp.sum(found, axis=1, keepdims=True), gate)
    gate_ref[...] = gate


def combine(pick, back, cotangent, slot_of):
    shape = jax.ShapeDtypeStruct(cotangent.shape, BF)
    return pl.pallas_call(
        combine_kernel,
        out_shape=(shape, shape, jax.ShapeDtypeStruct(slot_of.shape, F32)),
        in_specs=[VMEM] * 4,
        out_specs=(VMEM,) * 3,
        compiler_params=pltpu.CompilerParams(vmem_limit_bytes=8 * 2**20),
        cost_estimate=pl.CostEstimate(
            flops=128 * back.size, bytes_accessed=2 * back.size, transcendentals=0
        ),
    )(pick, back, cotangent, slot_of)


def shards(old_up, old_down, group_ids, freq_counts, tokens, routing, probs, cotangent):
    columns, depth = lax.axis_size("y"), lax.axis_size("z")
    chips = columns * depth
    groups = chips
    width = tokens.shape[1]
    token_rows, chosen = routing.shape
    block = width // chips
    quarter = old_up.shape[3]
    chip = ("y", "z")
    both = ("y", "z", "core")

    member = (group_ids[None, :] == jnp.arange(groups, dtype=jnp.int32)[:, None]).astype(jnp.int32)
    rank = jnp.sum((jnp.cumsum(member, axis=1) - member) * member, axis=0)
    weights = freq_counts.astype(F32)
    totals = jnp.sum(member.astype(F32) * weights[None, :], axis=1)
    merge_coef = member.astype(F32) * weights[None, :] / totals[:, None]
    select = member[:, None, :] * (
        rank[None, None, :] == jnp.arange(GMAX, dtype=jnp.int32)[None, :, None]
    ).astype(jnp.int32)
    index_table = jnp.sum(
        select * jnp.arange(member.shape[1], dtype=jnp.int32)[None, None, :], axis=2
    ).astype(jnp.int32)
    coef_table = jnp.sum(select.astype(F32) * merge_coef[:, None, :], axis=2)

    def by_owner(w):
        return w.reshape(chips, block, 2, quarter).transpose(0, 2, 1, 3)

    spread = jnp.concatenate([by_owner(old_up), by_owner(old_down)], axis=2)
    spread = spread.reshape(2 * chips, 2 * block, quarter)
    spread = lax.all_to_all(spread, both, split_axis=0, concat_axis=0, tiled=True)
    up_half, down_half = merge(index_table, coef_table, spread)
    up_half = lax.all_to_all(up_half, chip, split_axis=0, concat_axis=0, tiled=True)
    down_half, up_half = lax.optimization_barrier((down_half, up_half))
    w_up = lax.all_gather(up_half.reshape(width, quarter), "dp", axis=1, tiled=True)
    down_half = lax.all_to_all(down_half, chip, split_axis=0, concat_axis=0, tiled=True)
    w_down = lax.all_gather(down_half.reshape(width, quarter), "dp", axis=1, tiled=True)

    p_high = probs.astype(BF)
    p_rest = probs - p_high.astype(F32)
    p_mid = p_rest.astype(BF)
    p_low = (p_rest - p_mid.astype(F32)).astype(BF)
    notes = jnp.concatenate([routing.astype(BF), p_high, p_mid, p_low], axis=1)
    notes = jnp.pad(notes, ((0, 0), (0, LANES - notes.shape[1])))
    packed = jnp.concatenate([tokens, cotangent, notes], axis=1)
    column = lax.all_gather(packed, "z", axis=0, tiled=True)
    col_tokens = column[:, :width]
    col_cot = column[:, width : 2 * width]
    col_notes = column[:, 2 * width :].astype(F32)
    col_routing = col_notes[:, :chosen].astype(jnp.int32)
    col_p = col_notes[:, chosen : 2 * chosen] + col_notes[:, 2 * chosen : 3 * chosen]
    col_p = col_p + col_notes[:, 3 * chosen : 4 * chosen]

    count = depth * token_rows
    experts = jnp.arange(columns, dtype=jnp.int32) * depth + lax.axis_index("z")
    named = col_routing[None] == experts[:, None, None]
    names = jnp.any(named, axis=2).astype(jnp.int32)
    weight = jnp.sum(jnp.where(named, col_p[None], 0.0), axis=2)
    inside = names.reshape(columns, depth, token_rows)
    order = (jnp.cumsum(inside, axis=2) - inside).reshape(columns, count)
    source = jnp.arange(count, dtype=jnp.int32)[None, :] // token_rows
    row_at = (jnp.arange(columns, dtype=jnp.int32)[:, None] * depth + source) * (2 * SLOTS) + order
    row_at = jnp.where(names > 0, row_at, -2 * SLOTS)
    sent = columns * depth * 2 * SLOTS
    row_id = jnp.arange(sent, dtype=jnp.int32)
    hit_tok = row_id[:, None, None] == row_at[None]
    hit_cot = row_id[:, None, None] == row_at[None] + SLOTS
    pick = jnp.concatenate([jnp.any(hit_tok, axis=1), jnp.any(hit_cot, axis=1)], axis=1).astype(BF)
    row_p = jnp.sum(jnp.where(hit_cot, weight[None], 0.0), axis=(1, 2))
    factor = jnp.where((row_id // SLOTS) % 2 == 0, 1.0, row_p)
    send = jnp.dot(pick[:, :count], col_tokens, preferred_element_type=F32)
    send = send + jnp.dot(pick[:, count:], col_cot, preferred_element_type=F32)
    send = (send * factor[:, None]).astype(BF).reshape(columns, depth * 2 * SLOTS, width)
    send, down_half = lax.optimization_barrier((send, down_half))
    recv = lax.all_to_all(send, "y", split_axis=0, concat_axis=0, tiled=True)

    flat = routing.reshape(-1)
    onehot = (flat[:, None] == jnp.arange(groups, dtype=jnp.int32)[None, :]).astype(jnp.int32)
    order_rank = jnp.sum((jnp.cumsum(onehot, axis=0) - onehot) * onehot, axis=1)
    slot_of = (flat * (2 * SLOTS) + order_rank).reshape(token_rows, chosen)
    places = groups * 2 * SLOTS
    place = jnp.arange(places, dtype=jnp.int32)
    hit_x = place[:, None, None] == slot_of[None]
    hit_g = place[:, None, None] == slot_of[None] + SLOTS
    map_g = jnp.any(hit_g, axis=2).astype(BF)
    swap = [(0, 1), (1, 0)]
    per = chips * 2 * SLOTS
    recv = recv.reshape(per, width)
    other = lax.ppermute(recv, "core", swap)

    theirs, act_theirs, hid_theirs = expert(other, w_up, w_down)
    arrived = lax.ppermute(theirs, "core", swap)
    mine, act_mine, hid_mine = expert(recv, w_up, w_down)
    back, act_mine, hid_mine = lax.optimization_barrier((add_rows(mine, arrived), act_mine, hid_mine))
    back = back.reshape(groups, 2 * SLOTS, width)
    back = lax.all_to_all(back, chip, split_axis=0, concat_axis=0, tiled=True)
    back = back.reshape(places, width)
    up_share = over_dp(weight_part(act_mine, act_theirs, recv, other))
    down_share = over_dp(weight_part(hid_mine, hid_theirs, recv, other))

    with_p = jnp.sum(jnp.where(hit_x, probs[None], 0.0), axis=2).T
    p_high = with_p.astype(BF)
    p_low = (with_p - p_high.astype(F32)).astype(BF)
    gather = jnp.concatenate([p_high, p_low, map_g.T], axis=0)
    layer_out, token_grad, gate_grad = combine(gather, back, cotangent, slot_of)
    return layer_out, token_grad, gate_grad, up_share[None], down_share[None]


def solution(mesh):
    experts, data = mesh.devices.shape
    columns = data
    depth = experts // (2 * columns)
    fine = Mesh(mesh.devices.reshape(columns, depth, 2, data), ("y", "z", "core", "dp"))
    expert = ("y", "z", "core")
    rows = ("y", "z", "core", "dp")
    in_specs = (
        P(expert, None, None, "dp"),
        P(expert, None, None, "dp"),
        P(),
        P(),
        P(rows, None),
        P(rows, None),
        P(rows, None),
        P(rows, None),
    )
    out_specs = (
        P(rows, None),
        P(rows, None),
        P(rows, None),
        P(expert, None, "dp"),
        P(expert, None, "dp"),
    )
    return jax.shard_map(shards, mesh=fine, in_specs=in_specs, out_specs=out_specs, check_vma=False)
```

```python
import jax
import jax.numpy as jnp
from jax import lax
from jax.experimental import pallas as pl
from jax.experimental.pallas import tpu as pltpu
from jax.sharding import Mesh
from jax.sharding import PartitionSpec as P

GMAX = 3
LANES = 128
SLOTS = 4
BF = jnp.bfloat16
F32 = jnp.float32


def merge_kernel(index_ref, coef_ref, rows_ref, up_ref, down_ref):
    groups, block = up_ref.shape[:2]

    def one(g, carry):
        total = coef_ref[GMAX * g] * rows_ref[index_ref[GMAX * g]].astype(F32)
        for m in range(1, GMAX):
            total = total + coef_ref[GMAX * g + m] * rows_ref[index_ref[GMAX * g + m]].astype(F32)
        merged = total.astype(BF)
        up_ref[g] = merged[:block]
        down_ref[g] = merged[block:]
        return carry

    lax.fori_loop(0, groups, one, 0, unroll=4)


def merge(index_table, coef_table, rows):
    groups = index_table.shape[0]
    half = jax.ShapeDtypeStruct((groups, rows.shape[1] // 2, rows.shape[2]), BF)
    vmem = pl.BlockSpec(memory_space=pltpu.VMEM)
    return pl.pallas_call(
        merge_kernel,
        out_shape=(half, half),
        in_specs=[
            pl.BlockSpec(memory_space=pltpu.SMEM),
            pl.BlockSpec(memory_space=pltpu.SMEM),
            vmem,
        ],
        out_specs=(vmem, vmem),
        compiler_params=pltpu.CompilerParams(vmem_limit_bytes=24 * 2**20),
        cost_estimate=pl.CostEstimate(
            flops=0, bytes_accessed=2 * rows.size + 4 * half.size, transcendentals=0
        ),
    )(index_table.reshape(-1), coef_table.reshape(-1), rows)


VMEM = pl.BlockSpec(memory_space=pltpu.VMEM)
TILE = 256
LAST = (((1,), (1,)), ((), ()))


def expert_kernel(rows_ref, up_ref, down_ref, out_ref, act_ref, hid_ref):
    rows = rows_ref[...]
    count = rows.shape[0]
    preact = jnp.dot(rows, up_ref[...], preferred_element_type=F32)
    hidden_grad = jnp.dot(rows, down_ref[...], preferred_element_type=F32)
    is_x = lax.broadcasted_iota(jnp.int32, preact.shape, 0) % (2 * SLOTS) < SLOTS
    sig = jax.nn.sigmoid(preact)
    slope = sig * (1.0 + preact * (1.0 - sig))
    hidden = jnp.where(is_x, preact * sig, 0.0)
    act_grad = jnp.where(is_x, pltpu.roll(hidden_grad, count - SLOTS, 0) * slope, 0.0)
    last = (((1,), (1,)), ((), ()))
    result = lax.dot_general(hidden.astype(BF), down_ref[...], last, preferred_element_type=F32)
    act_at_g = pltpu.roll(act_grad, SLOTS, 0).astype(BF)
    result = result + lax.dot_general(act_at_g, up_ref[...], last, preferred_element_type=F32)
    out_ref[...] = result.astype(BF)
    act_ref[...] = act_grad.T.astype(BF)
    hid_ref[...] = pltpu.roll(hidden, SLOTS, 0).T.astype(BF)


def expert(rows, w_up, w_down):
    count, width = rows.shape
    units = w_up.shape[1]
    tile = 512
    whole = pl.BlockSpec((width, units), lambda i: (0, 0))
    return pl.pallas_call(
        expert_kernel,
        grid=(count // tile,),
        out_shape=(
            jax.ShapeDtypeStruct((count, width), BF),
            jax.ShapeDtypeStruct((units, count), BF),
            jax.ShapeDtypeStruct((units, count), BF),
        ),
        in_specs=[pl.BlockSpec((tile, width), lambda i: (i, 0)), whole, whole],
        out_specs=(
            pl.BlockSpec((tile, width), lambda i: (i, 0)),
            pl.BlockSpec((units, tile), lambda i: (0, i)),
            pl.BlockSpec((units, tile), lambda i: (0, i)),
        ),
        compiler_params=pltpu.CompilerParams(vmem_limit_bytes=48 * 2**20),
        cost_estimate=pl.CostEstimate(
            flops=8 * count * width * units,
            bytes_accessed=4 * count * width + 4 * width * units + 4 * units * count,
            transcendentals=count * units,
        ),
    )(rows, w_up, w_down)


def add_kernel(mine_ref, theirs_ref, out_ref):
    out_ref[...] = (mine_ref[...].astype(F32) + theirs_ref[...].astype(F32)).astype(BF)


def add_rows(mine, theirs):
    return pl.pallas_call(
        add_kernel,
        out_shape=jax.ShapeDtypeStruct(mine.shape, BF),
        in_specs=[VMEM] * 2,
        out_specs=VMEM,
        compiler_params=pltpu.CompilerParams(vmem_limit_bytes=12 * 2**20),
        cost_estimate=pl.CostEstimate(
            flops=mine.size, bytes_accessed=6 * mine.size, transcendentals=0
        ),
    )(mine, theirs)


def grad_kernel(mine_ref, theirs_ref, recv_ref, other_ref, out_ref):
    for start in range(0, recv_ref.shape[1], 2 * TILE):
        at = pl.ds(start, 2 * TILE)
        part = jnp.dot(mine_ref[...], recv_ref[:, at], preferred_element_type=F32)
        part = part + jnp.dot(theirs_ref[...], other_ref[:, at], preferred_element_type=F32)
        out_ref[:, at] = part.astype(BF)


def weight_part(left_mine, left_theirs, recv, other):
    units, count = left_mine.shape
    width = recv.shape[1]
    return pl.pallas_call(
        grad_kernel,
        out_shape=jax.ShapeDtypeStruct((units, width), BF),
        in_specs=[VMEM] * 4,
        out_specs=VMEM,
        compiler_params=pltpu.CompilerParams(vmem_limit_bytes=12 * 2**20),
        cost_estimate=pl.CostEstimate(
            flops=4 * count * width * units,
            bytes_accessed=4 * count * width + 4 * units * count + 2 * units * width,
            transcendentals=0,
        ),
    )(left_mine, left_theirs, recv, other)


def over_dp(part):
    return lax.psum_scatter(part, "dp", scatter_dimension=0, tiled=True).T


def combine_kernel(pick_ref, back_ref, cot_ref, slot_ref, layer_ref, token_ref, gate_ref):
    tokens, chosen = slot_ref.shape
    back = back_ref[...]
    sums = jnp.dot(pick_ref[...], back, preferred_element_type=F32)
    layer_ref[...] = (sums[:tokens] + sums[tokens : 2 * tokens]).astype(BF)
    token_ref[...] = sums[2 * tokens :].astype(BF)
    gates = lax.dot_general(cot_ref[...], back, LAST, preferred_element_type=F32)
    place = lax.broadcasted_iota(jnp.int32, gates.shape, 1)
    column = lax.broadcasted_iota(jnp.int32, (tokens, chosen), 1)
    gate = jnp.zeros((tokens, chosen), F32)
    for k in range(chosen):
        found = jnp.where(place == slot_ref[:, k : k + 1], gates, 0.0)
        gate = jnp.where(column == k, jnp.sum(found, axis=1, keepdims=True), gate)
    gate_ref[...] = gate


def combine(pick, back, cotangent, slot_of):
    shape = jax.ShapeDtypeStruct(cotangent.shape, BF)
    return pl.pallas_call(
        combine_kernel,
        out_shape=(shape, shape, jax.ShapeDtypeStruct(slot_of.shape, F32)),
        in_specs=[VMEM] * 4,
        out_specs=(VMEM,) * 3,
        compiler_params=pltpu.CompilerParams(vmem_limit_bytes=8 * 2**20),
        cost_estimate=pl.CostEstimate(
            flops=128 * back.size, bytes_accessed=2 * back.size, transcendentals=0
        ),
    )(pick, back, cotangent, slot_of)


def shards(old_up, old_down, group_ids, freq_counts, tokens, routing, probs, cotangent):
    columns, depth = lax.axis_size("y"), lax.axis_size("z")
    chips = columns * depth
    groups = chips
    width = tokens.shape[1]
    token_rows, chosen = routing.shape
    block = width // chips
    quarter = old_up.shape[3]
    chip = ("y", "z")
    both = ("y", "z", "core")

    member = (group_ids[None, :] == jnp.arange(groups, dtype=jnp.int32)[:, None]).astype(jnp.int32)
    rank = jnp.sum((jnp.cumsum(member, axis=1) - member) * member, axis=0)
    weights = freq_counts.astype(F32)
    totals = jnp.sum(member.astype(F32) * weights[None, :], axis=1)
    merge_coef = member.astype(F32) * weights[None, :] / totals[:, None]
    select = member[:, None, :] * (
        rank[None, None, :] == jnp.arange(GMAX, dtype=jnp.int32)[None, :, None]
    ).astype(jnp.int32)
    index_table = jnp.sum(
        select * jnp.arange(member.shape[1], dtype=jnp.int32)[None, None, :], axis=2
    ).astype(jnp.int32)
    coef_table = jnp.sum(select.astype(F32) * merge_coef[:, None, :], axis=2)

    def by_owner(w):
        return w.reshape(chips, block, 2, quarter).transpose(0, 2, 1, 3)

    spread = jnp.concatenate([by_owner(old_up), by_owner(old_down)], axis=2)
    spread = spread.reshape(2 * chips, 2 * block, quarter)
    spread = lax.all_to_all(spread, both, split_axis=0, concat_axis=0, tiled=True)
    up_half, down_half = merge(index_table, coef_table, spread)
    up_half = lax.all_to_all(up_half, chip, split_axis=0, concat_axis=0, tiled=True)
    down_half, up_half = lax.optimization_barrier((down_half, up_half))
    w_up = lax.all_gather(up_half.reshape(width, quarter), "dp", axis=1, tiled=True)
    down_half = lax.all_to_all(down_half, chip, split_axis=0, concat_axis=0, tiled=True)
    w_down = lax.all_gather(down_half.reshape(width, quarter), "dp", axis=1, tiled=True)

    p_high = probs.astype(BF)
    p_rest = probs - p_high.astype(F32)
    p_mid = p_rest.astype(BF)
    p_low = (p_rest - p_mid.astype(F32)).astype(BF)
    notes = jnp.concatenate([routing.astype(BF), p_high, p_mid, p_low], axis=1)
    notes = jnp.pad(notes, ((0, 0), (0, LANES - notes.shape[1])))
    packed = jnp.concatenate([tokens, cotangent, notes], axis=1)
    column = lax.all_gather(packed, "z", axis=0, tiled=True)
    col_tokens = column[:, :width]
    col_cot = column[:, width : 2 * width]
    col_notes = column[:, 2 * width :].astype(F32)
    col_routing = col_notes[:, :chosen].astype(jnp.int32)
    col_p = col_notes[:, chosen : 2 * chosen] + col_notes[:, 2 * chosen : 3 * chosen]
    col_p = col_p + col_notes[:, 3 * chosen : 4 * chosen]

    count = depth * token_rows
    experts = jnp.arange(columns, dtype=jnp.int32) * depth + lax.axis_index("z")
    named = col_routing[None] == experts[:, None, None]
    names = jnp.any(named, axis=2).astype(jnp.int32)
    weight = jnp.sum(jnp.where(named, col_p[None], 0.0), axis=2)
    inside = names.reshape(columns, depth, token_rows)
    order = (jnp.cumsum(inside, axis=2) - inside).reshape(columns, count)
    source = jnp.arange(count, dtype=jnp.int32)[None, :] // token_rows
    row_at = (jnp.arange(columns, dtype=jnp.int32)[:, None] * depth + source) * (2 * SLOTS) + order
    row_at = jnp.where(names > 0, row_at, -2 * SLOTS)
    sent = columns * depth * 2 * SLOTS
    row_id = jnp.arange(sent, dtype=jnp.int32)
    hit_tok = row_id[:, None, None] == row_at[None]
    hit_cot = row_id[:, None, None] == row_at[None] + SLOTS
    pick = jnp.concatenate([jnp.any(hit_tok, axis=1), jnp.any(hit_cot, axis=1)], axis=1).astype(BF)
    row_p = jnp.sum(jnp.where(hit_cot, weight[None], 0.0), axis=(1, 2))
    factor = jnp.where((row_id // SLOTS) % 2 == 0, 1.0, row_p)
    send = jnp.dot(pick[:, :count], col_tokens, preferred_element_type=F32)
    send = send + jnp.dot(pick[:, count:], col_cot, preferred_element_type=F32)
    send = (send * factor[:, None]).astype(BF).reshape(columns, depth * 2 * SLOTS, width)
    send, down_half = lax.optimization_barrier((send, down_half))
    recv = lax.all_to_all(send, "y", split_axis=0, concat_axis=0, tiled=True)

    flat = routing.reshape(-1)
    onehot = (flat[:, None] == jnp.arange(groups, dtype=jnp.int32)[None, :]).astype(jnp.int32)
    order_rank = jnp.sum((jnp.cumsum(onehot, axis=0) - onehot) * onehot, axis=1)
    slot_of = (flat * (2 * SLOTS) + order_rank).reshape(token_rows, chosen)
    places = groups * 2 * SLOTS
    place = jnp.arange(places, dtype=jnp.int32)
    hit_x = place[:, None, None] == slot_of[None]
    hit_g = place[:, None, None] == slot_of[None] + SLOTS
    map_g = jnp.any(hit_g, axis=2).astype(BF)
    swap = [(0, 1), (1, 0)]
    per = chips * 2 * SLOTS
    recv = recv.reshape(per, width)
    other = lax.ppermute(recv, "core", swap)

    theirs, act_theirs, hid_theirs = expert(other, w_up, w_down)
    arrived = lax.ppermute(theirs, "core", swap)
    mine, act_mine, hid_mine = expert(recv, w_up, w_down)
    back, act_mine, hid_mine = lax.optimization_barrier((add_rows(mine, arrived), act_mine, hid_mine))
    back = back.reshape(groups, 2 * SLOTS, width)
    back = lax.all_to_all(back, chip, split_axis=0, concat_axis=0, tiled=True)
    back = back.reshape(places, width)
    up_share = over_dp(weight_part(act_mine, act_theirs, recv, other))
    down_share = over_dp(weight_part(hid_mine, hid_theirs, recv, other))

    with_p = jnp.sum(jnp.where(hit_x, probs[None], 0.0), axis=2).T
    p_high = with_p.astype(BF)
    p_low = (with_p - p_high.astype(F32)).astype(BF)
    gather = jnp.concatenate([p_high, p_low, map_g.T], axis=0)
    layer_out, token_grad, gate_grad = combine(gather, back, cotangent, slot_of)
    return layer_out, token_grad, gate_grad, up_share[None], down_share[None]


def solution(mesh):
    experts, data = mesh.devices.shape
    columns = data
    depth = experts // (2 * columns)
    fine = Mesh(mesh.devices.reshape(columns, depth, 2, data), ("y", "z", "core", "dp"))
    expert = ("y", "z", "core")
    rows = ("y", "z", "core", "dp")
    in_specs = (
        P(expert, None, None, "dp"),
        P(expert, None, None, "dp"),
        P(),
        P(),
        P(rows, None),
        P(rows, None),
        P(rows, None),
        P(rows, None),
    )
    out_specs = (
        P(rows, None),
        P(rows, None),
        P(rows, None),
        P(expert, None, "dp"),
        P(expert, None, "dp"),
    )
    return jax.shard_map(shards, mesh=fine, in_specs=in_specs, out_specs=out_specs, check_vma=False)
```
